32 devices in a mesh: orb: 8 (over z, core), bas: 4 (over y, x).
Axes of the slice: x: 2, y: 2, z: 4, core: 2. Of those that a mesh axis runs over, the one named last changes fastest.
Arguments:
- coeffs: bfloat16 [131072, 1024], P('bas', 'orb'), may hold values from -6 to 6
- dipole: bfloat16 [3, 4, 32768, 384], P(None, 'bas', 'orb'), may hold values from -0.0008544922 to 0.0008544922
- tile_cols: int32 [4, 256, 3], P('bas', 'orb'), may hold values from -1 to 31, as said below
- matching: int32 [1, 8], replicated, may hold values from 0 to 7, as said below
Outputs:
- localized: bfloat16 [131072, 1024], P('bas', 'orb')
The draws below stay inside these ranges and needn't reach their ends.
Inputs may be any that keep to these rules, and one draw needn't show every extreme that they name: `tile_cols`: entry [b, r, s] is the column tile of slot s of row tile r of basis block b, counted within the row tile's group of 32 tiles, or -1 for a padded slot; slot 0 is the row tile itself, and the live slots of a row name distinct tiles. `matching`: each row pairs every block with another block and is its own inverse; the rows are distinct rounds of one round-robin tournament.
All inputs are finite; a program needn't handle non-finite values.
Results may differ from the reference program's by a relative error of at most 0.0047.
Values may be sent and summed in bfloat16 or wider, within the bound.
A program may use at most 192 MiB of HBM per device.

```python
import jax
import jax.numpy as jnp
from jax import lax

NBAS = 131072
BLK = 128
TILE = 128
SLOTS = 3
SWEEPS = 4
ROUNDS = 1
NBLK = 8
NORB = 1024
BROWS = 32768
ROWT = 256
GROUP = 32
N_ORB = 8
N_BAS = 4


def draw_tile_cols(key, part):
    row_total = N_BAS * ROWT
    key_one, key_two, key_three = jax.random.split(key, 3)
    local_tile = jnp.arange(row_total, dtype=jnp.int32) % GROUP
    step_one = jax.random.randint(key_one, (row_total,), 1, GROUP)
    step_two = 1 + (step_one - 1 + jax.random.randint(key_two, (row_total,), 1, GROUP - 1)) % (GROUP - 1)
    alive = jax.random.randint(key_three, (row_total, 2), 0, 4) > 0
    slot_one = jnp.where(alive[:, 0], (local_tile + step_one) % GROUP, -1)
    slot_two = jnp.where(alive[:, 1], (local_tile + step_two) % GROUP, -1)
    table = jnp.stack([local_tile, slot_one, slot_two], axis=-1)
    return table.reshape(N_BAS, ROWT, SLOTS).astype(jnp.int32)


def draw_matching(key, part):
    players = NBLK
    key_one, key_two = jax.random.split(key)
    labels = jax.random.permutation(key_one, players).astype(jnp.int32)
    chosen = jax.random.permutation(key_two, players - 1).astype(jnp.int32)
    indices = jnp.arange(players - 1, dtype=jnp.int32)
    tables = []
    for round_index in range(ROUNDS):
        pick = chosen[round_index]
        opposite = (2 * pick - indices) % (players - 1)
        partner_small = jnp.where(opposite == indices, players - 1, opposite)
        partner_full = jnp.concatenate([partner_small, pick[None]]).astype(jnp.int32)
        mapped = jnp.zeros((players,), jnp.int32).at[labels].set(labels[partner_full])
        tables.append(mapped)
    return jnp.stack(tables).astype(jnp.int32)


def steps_of(key, dims, cuts, least, high):
    def one(axis_at, parts):
        steps = jax.random.uniform(jax.random.fold_in(jax.random.fold_in(key, 6), axis_at), (parts,), jnp.float32, least / len(cuts), high / len(cuts))
        return jnp.repeat(jnp.exp(steps), dims[axis_at] // parts).reshape((-1,) + (1,) * (len(dims) - axis_at - 1))

    level = one(*cuts[0])
    for cut in cuts[1:]:
        level = level * one(*cut)
    return level


def gaussian(stream_key, extent, scale, reach, pieces=(), kind=jnp.bfloat16):
    entries = jax.random.normal(stream_key, extent, jnp.float32) * scale
    if len(pieces) > 0:
        entries = steps_of(stream_key, extent, pieces, -0.22, 0.18) * entries
    return jnp.clip(entries, min=-reach, max=reach).astype(kind)


def setup_inputs(seed: int = 0) -> dict:
    key_list = jax.random.split(jax.random.key(seed), 5)
    coeffs = gaussian(key_list[0], (NBAS, NORB), 1.0, 6.0, ((0, 4), (1, 8)))
    dipole = gaussian(key_list[1], (3, N_BAS, BROWS, SLOTS * TILE), (NBAS * SLOTS * TILE) ** -0.5, 0.0008544922, ((1, 4), (2, 8)))
    tile_cols = draw_tile_cols(jax.random.fold_in(key_list[4], 71), 0)
    matching = draw_matching(jax.random.fold_in(key_list[4], 71), 0)
    return {"coeffs": coeffs, "dipole": dipole, "tile_cols": tile_cols, "matching": matching}


def jacobi_pair(gram):
    highest = lax.Precision.HIGHEST
    half = gram.shape[1] // 2
    positions = jnp.arange(half, dtype=jnp.int32)
    accum = jnp.eye(2 * half, dtype=jnp.float32)
    for sweep_index in range(SWEEPS):
        permute = jnp.equal(positions[None, :], (positions[:, None] + sweep_index) % half).astype(jnp.float32)
        diag_vals = jnp.diagonal(gram, axis1=1, axis2=2)
        head_vals = diag_vals[:, :half]
        tail_vals = jnp.roll(diag_vals[:, half:], -sweep_index, axis=1)
        off_vals = jnp.diagonal(jnp.roll(gram[:, :half, half:], -sweep_index, axis=2), axis1=1, axis2=2)
        spread = head_vals - tail_vals
        quad_term = jnp.sum(off_vals * off_vals - 0.25 * spread * spread, axis=0)
        lin_term = jnp.sum(off_vals * spread, axis=0)
        angles = 0.25 * jnp.arctan(lin_term / (jnp.abs(quad_term) + 1.0))
        cosine = jnp.cos(angles)
        sine_part = jnp.sin(angles)
        upper_half = jnp.concatenate([jnp.diag(cosine), -(sine_part[:, None] * permute)], axis=1)
        bottom = jnp.concatenate([permute.T * sine_part[None, :], jnp.diag(jnp.roll(cosine, sweep_index))], axis=1)
        rotation = jnp.concatenate([upper_half, bottom], axis=0)
        gram = jnp.einsum("ji,kjl->kil", rotation, jnp.einsum("kij,jl->kil", gram, rotation, precision=highest), precision=highest)
        accum = jnp.dot(accum, rotation, precision=highest)
    return accum


def project_rows(dipole_group, tile_index, group_rows):
    tile_rows = group_rows.reshape(GROUP, TILE, NORB)
    picked = tile_rows[jnp.maximum(tile_index, 0)]
    picked = jnp.where((tile_index >= 0)[:, :, None, None], picked, jnp.zeros_like(picked))
    picked = picked.reshape(GROUP, SLOTS * TILE, NORB)
    moments = jnp.einsum("kraj,rjn->kran", dipole_group.astype(jnp.float32), picked.astype(jnp.float32)).astype(jnp.bfloat16)
    return moments.reshape(3, GROUP * TILE, NBLK, BLK)


def gram_terms(coef_blocks, moment_blocks, leader, follower):
    coef_wide = coef_blocks.astype(jnp.float32)
    moment_wide = moment_blocks.astype(jnp.float32)
    raw_gram = jnp.einsum("rbi,krbj->bkij", coef_wide, moment_wide)
    self_gram = 0.5 * (raw_gram + jnp.swapaxes(raw_gram, 2, 3))
    cross_one = jnp.einsum("rbi,krbj->bkij", coef_wide[:, leader], moment_wide[:, :, follower])
    cross_two = jnp.einsum("krbi,rbj->bkij", moment_wide[:, :, leader], coef_wide[:, follower])
    return self_gram, 0.5 * (cross_one + cross_two)


def rotate_rows(group_rows, weights, leader, follower):
    coef_blocks = group_rows.reshape(group_rows.shape[0], NBLK, BLK)
    paired = jnp.concatenate([coef_blocks[:, leader], coef_blocks[:, follower]], axis=2)
    rotated = jnp.einsum("rbj,bjn->rbn", paired.astype(jnp.float32), weights.astype(jnp.float32))
    return rotated.astype(jnp.bfloat16).reshape(group_rows.shape[0], NORB)


def reference(coeffs, dipole, tile_cols, matching):
    groups = N_BAS * N_ORB
    dipole_groups = jnp.moveaxis(dipole.reshape(3, groups, GROUP, TILE, SLOTS * TILE), 1, 0)
    tile_groups = tile_cols.reshape(groups, GROUP, SLOTS)
    row_groups = coeffs.reshape(groups, GROUP * TILE, NORB)
    block_ids = jnp.arange(NBLK, dtype=jnp.int32)
    for round_index in range(ROUNDS):
        partner = matching[round_index]
        leader = jnp.minimum(block_ids, partner)
        follower = jnp.maximum(block_ids, partner)

        def add_group(totals, inputs):
            dipole_group, tile_index, group_rows = inputs
            moments = project_rows(dipole_group, tile_index, group_rows)
            self_gram, cross_gram = gram_terms(group_rows.reshape(GROUP * TILE, NBLK, BLK), moments, leader, follower)
            return (totals[0] + self_gram, totals[1] + cross_gram), None

        zeros_init = jnp.zeros((NBLK, 3, BLK, BLK), jnp.float32)
        (self_gram, cross_gram), unused = lax.scan(add_group, (zeros_init, zeros_init), (dipole_groups, tile_groups, row_groups))
        upper_half = jnp.concatenate([self_gram[leader], cross_gram], axis=3)
        lower_half = jnp.concatenate([jnp.swapaxes(cross_gram, 2, 3), self_gram[follower]], axis=3)
        pair_gram = jnp.concatenate([upper_half, lower_half], axis=2)
        rotors = jax.vmap(jacobi_pair)(pair_gram)
        weights = jnp.where((leader == block_ids)[:, None, None], rotors[:, :, :BLK], rotors[:, :, BLK:]).astype(jnp.bfloat16)

        def rotate_group(group_rows):
            return rotate_rows(group_rows, weights, leader, follower)

        row_groups = lax.map(rotate_group, row_groups)
    return row_groups.reshape(NBAS, NORB)
```

```python
import functools

import jax
import jax.numpy as jnp
from jax import lax
from jax.experimental import pallas as pl
from jax.experimental.pallas import tpu as pltpu
from jax.sharding import PartitionSpec as P

SWEEPS = 4
VMEM_LIMIT = 56 * 1024 * 1024


def permute_kernel(index_ref, in_ref, out_ref):
    out_ref[...] = in_ref[...]


def permute_blocks(blocks, index):
    count, rows, cols = blocks.shape
    return pl.pallas_call(
        permute_kernel,
        out_shape=jax.ShapeDtypeStruct(blocks.shape, blocks.dtype),
        grid_spec=pltpu.PrefetchScalarGridSpec(
            num_scalar_prefetch=1,
            grid=(count,),
            in_specs=[pl.BlockSpec((1, rows, cols), lambda o, index: (index[o], 0, 0))],
            out_specs=pl.BlockSpec((1, rows, cols), lambda o, index: (o, 0, 0)),
        ),
        cost_estimate=pl.CostEstimate(
            flops=0, bytes_accessed=2 * blocks.size * 2, transcendentals=0
        ),
    )(index, blocks)


def pair_kernel(
    tiles, slots, leads, follows, table, lead_ref, follow_ref, dipole_ref, out_ref, x_ref, xt_ref, m_ref
):
    tile = lead_ref.shape[1] // tiles
    half = lead_ref.shape[2]
    x_ref[:, :half] = lead_ref[0]
    x_ref[:, half:] = follow_ref[0]

    def project(r, carry):
        rows = pl.ds(pl.multiple_of(r * tile, tile), tile)
        picked = []
        for s in range(slots):
            col = table[r * slots + s]
            start = pl.multiple_of(jnp.maximum(col, 0) * tile, tile)
            piece = x_ref[pl.ds(start, tile), :]
            picked.append(jnp.where(col >= 0, piece, jnp.zeros_like(piece)))
        picked = jnp.concatenate(picked, axis=0)
        for k in range(3):
            m_ref[k, rows, :] = jnp.dot(
                dipole_ref[k, rows, :], picked, preferred_element_type=jnp.float32
            ).astype(jnp.bfloat16)
        xt_ref[:, rows] = x_ref[rows, :].T
        return carry

    lax.fori_loop(0, tiles, project, 0)
    for k in range(3):
        out_ref[0, k] = jnp.dot(xt_ref[...], m_ref[k], preferred_element_type=jnp.float32)


def pair_grams(local, dipole, table, leads, follows):
    blocks, rows, half = local.shape
    tiles, slots = table.shape
    pairs = blocks // 2
    flops = pairs * 2 * 3 * rows * 2 * half * (dipole.shape[2] + 2 * half)
    return pl.pallas_call(
        functools.partial(pair_kernel, tiles, slots),
        out_shape=jax.ShapeDtypeStruct((pairs, 3, 2 * half, 2 * half), jnp.float32),
        grid_spec=pltpu.PrefetchScalarGridSpec(
            num_scalar_prefetch=3,
            grid=(pairs,),
            in_specs=[
                pl.BlockSpec((1, rows, half), lambda q, lead, follow, t: (lead[q], 0, 0)),
                pl.BlockSpec((1, rows, half), lambda q, lead, follow, t: (follow[q], 0, 0)),
                pl.BlockSpec(dipole.shape, lambda q, lead, follow, t: (0, 0, 0)),
            ],
            out_specs=pl.BlockSpec(
                (1, 3, 2 * half, 2 * half), lambda q, lead, follow, t: (q, 0, 0, 0)
            ),
            scratch_shapes=[
                pltpu.VMEM((rows, 2 * half), jnp.bfloat16),
                pltpu.VMEM((2 * half, rows), jnp.bfloat16),
                pltpu.VMEM((3, rows, 2 * half), jnp.bfloat16),
            ],
        ),
        compiler_params=pltpu.CompilerParams(vmem_limit_bytes=VMEM_LIMIT),
        cost_estimate=pl.CostEstimate(
            flops=flops, bytes_accessed=2 * (local.size + dipole.size), transcendentals=0
        ),
    )(leads, follows, table.reshape(-1), local, local, dipole)


def arctan(x):
    mag = jnp.abs(x)
    big = mag > 2.414213562373095
    mid = mag > 0.4142135623730950
    num = jnp.where(big, -1.0, jnp.where(mid, mag - 1.0, mag))
    den = jnp.where(big, mag, jnp.where(mid, mag + 1.0, 1.0))
    base = jnp.where(big, 1.5707963267948966, jnp.where(mid, 0.7853981633974483, 0.0))
    t = num / den
    w = t * t
    poly = ((8.05374449538e-2 * w - 1.38776856032e-1) * w + 1.99777106478e-1) * w
    poly = (poly - 3.33329491539e-1) * w * t + t
    out = base + poly
    return jnp.where(x < 0, -out, out)


def jacobi_kernel(in_ref, out_ref):
    half = in_ref.shape[2] // 2
    rows = lax.broadcasted_iota(jnp.int32, (half, half), 0)
    cols = lax.broadcasted_iota(jnp.int32, (half, half), 1)
    eye = rows == cols
    quads = []
    for k in range(3):
        full = in_ref[0, k]
        full = 0.5 * (full + full.T)
        quads.append(
            [full[:half, :half], full[:half, half:], full[half:, :half], full[half:, half:]]
        )
    one = jnp.where(eye, 1.0, 0.0).astype(jnp.float32)
    zero = jnp.zeros((half, half), jnp.float32)
    rotor = [one, zero, zero, one]

    def angles(axis):
        quad_term = lin_term = 0.0
        for ll, lf, _, ff in quads:
            head, off, tail = (
                jnp.sum(jnp.where(eye, v, 0.0), axis=axis, keepdims=True) for v in (ll, lf, ff)
            )
            spread = head - tail
            quad_term = quad_term + (off * off - 0.25 * spread * spread)
            lin_term = lin_term + off * spread
        theta = 0.25 * arctan(lin_term / (jnp.abs(quad_term) + 1.0))
        return jnp.cos(theta), jnp.sin(theta)

    for sweep in range(SWEEPS):
        if sweep:
            back = half - 1
            for q in quads:
                q[1] = pltpu.roll(q[1], back, 1)
                q[2] = pltpu.roll(q[2], back, 0)
                q[3] = pltpu.roll(pltpu.roll(q[3], back, 1), back, 0)
            rotor[1] = pltpu.roll(rotor[1], back, 1)
            rotor[3] = pltpu.roll(rotor[3], back, 1)
        row_cos, row_sin = angles(0)
        col_cos, col_sin = angles(1)
        for i, (ll, lf, fl, ff) in enumerate(quads):
            ll, lf = ll * row_cos + lf * row_sin, lf * row_cos - ll * row_sin
            fl, ff = fl * row_cos + ff * row_sin, ff * row_cos - fl * row_sin
            ll, fl = ll * col_cos + fl * col_sin, fl * col_cos - ll * col_sin
            lf, ff = lf * col_cos + ff * col_sin, ff * col_cos - lf * col_sin
            quads[i] = [ll, lf, fl, ff]
        ll, lf, fl, ff = rotor
        rotor = [
            ll * row_cos + lf * row_sin,
            lf * row_cos - ll * row_sin,
            fl * row_cos + ff * row_sin,
            ff * row_cos - fl * row_sin,
        ]
    lf, ff = (pltpu.roll(v, SWEEPS - 1, 1) for v in (rotor[1], rotor[3]))
    out_ref[0, :half, :half] = rotor[0].astype(jnp.bfloat16)
    out_ref[0, half:, :half] = rotor[2].astype(jnp.bfloat16)
    out_ref[0, :half, half:] = lf.astype(jnp.bfloat16)
    out_ref[0, half:, half:] = ff.astype(jnp.bfloat16)


def jacobi(grams):
    pairs, _, size, _ = grams.shape
    return pl.pallas_call(
        jacobi_kernel,
        out_shape=jax.ShapeDtypeStruct((pairs, size, size), jnp.bfloat16),
        grid=(pairs,),
        in_specs=[pl.BlockSpec((1, 3, size, size), lambda q: (q, 0, 0, 0))],
        out_specs=pl.BlockSpec((1, size, size), lambda q: (q, 0, 0)),
        compiler_params=pltpu.CompilerParams(vmem_limit_bytes=32 * 1024 * 1024),
        cost_estimate=pl.CostEstimate(
            flops=pairs * SWEEPS * 3 * 12 * size * size,
            bytes_accessed=grams.size * 4,
            transcendentals=pairs * SWEEPS * 4 * size,
        ),
    )(grams)


def rotate_kernel(own_ref, other_ref, weight_ref, out_ref):
    both = jnp.concatenate([own_ref[...], other_ref[...]], axis=1)
    out_ref[...] = jnp.dot(both, weight_ref[...], preferred_element_type=jnp.float32).astype(
        jnp.bfloat16
    )


def rotate(own, other, weight):
    rows, half = own.shape
    step = min(rows, 4096)
    return pl.pallas_call(
        rotate_kernel,
        out_shape=jax.ShapeDtypeStruct(own.shape, own.dtype),
        grid=(rows // step,),
        in_specs=[
            pl.BlockSpec((step, half), lambda i: (i, 0)),
            pl.BlockSpec((step, half), lambda i: (i, 0)),
            pl.BlockSpec((2 * half, half), lambda i: (0, 0)),
        ],
        out_specs=pl.BlockSpec((step, half), lambda i: (i, 0)),
        compiler_params=pltpu.CompilerParams(vmem_limit_bytes=32 * 1024 * 1024),
        cost_estimate=pl.CostEstimate(
            flops=4 * rows * half * half, bytes_accessed=6 * own.size, transcendentals=0
        ),
    )(own, other, weight)


def body(coeffs, dipole, tile_cols, matching):
    blocks = lax.axis_size("orb")
    me = lax.axis_index("orb")
    rows, half = coeffs.shape
    pairs = blocks // 2
    block_ids = jnp.arange(blocks, dtype=jnp.int32)
    partner = matching[0]
    is_lead = block_ids < partner
    before = is_lead[None, :] & (block_ids[None, :] < block_ids[:, None])
    rank = jnp.sum(before.astype(jnp.int32), axis=1)
    chosen = is_lead[None, :] & (rank[None, :] == jnp.arange(pairs, dtype=jnp.int32)[:, None])
    leads = jnp.sum(jnp.where(chosen, block_ids[None, :], 0), axis=1)
    follows = jnp.sum(jnp.where(chosen, partner[None, :], 0), axis=1)

    local = lax.all_to_all(
        coeffs.reshape(blocks, rows // blocks, half), "orb", split_axis=0, concat_axis=0
    )
    swapped = permute_blocks(local, partner)
    other = lax.all_to_all(swapped, "orb", split_axis=0, concat_axis=0).reshape(rows, half)

    grams = pair_grams(local, dipole[:, 0], tile_cols[0], leads, follows)
    grams = lax.psum_scatter(grams, "bas", scatter_dimension=0, tiled=True)
    grams = lax.psum(grams, "orb")
    rotors = lax.all_gather(jacobi(grams), "bas", axis=0, tiled=True)
    mine = (leads == me) | (follows == me)
    rotor = jnp.sum(jnp.where(mine[:, None, None], rotors, jnp.zeros_like(rotors)), axis=0)
    leading = jnp.any(leads == me)
    weight = jnp.where(
        leading,
        rotor[:, :half],
        jnp.concatenate([rotor[half:, half:], rotor[:half, half:]], axis=0),
    )
    return rotate(coeffs, other, weight)


def solution(mesh):
    in_specs = (P("bas", "orb"), P(None, "bas", "orb", None), P("bas", "orb", None), P())
    out_specs = P("bas", "orb")
    return jax.shard_map(body, mesh=mesh, in_specs=in_specs, out_specs=out_specs, check_vma=False)
```

```python
import functools

import jax
import jax.numpy as jnp
from jax import lax
from jax.experimental import pallas as pl
from jax.experimental.pallas import tpu as pltpu
from jax.sharding import PartitionSpec as P

SWEEPS = 4
VMEM_LIMIT = 56 * 1024 * 1024


def permute_kernel(index_ref, in_ref, out_ref):
    out_ref[...] = in_ref[...]


def permute_blocks(blocks, index):
    count, rows, cols = blocks.shape
    return pl.pallas_call(
        permute_kernel,
        out_shape=jax.ShapeDtypeStruct(blocks.shape, blocks.dtype),
        grid_spec=pltpu.PrefetchScalarGridSpec(
            num_scalar_prefetch=1,
            grid=(count, 2),
            in_specs=[pl.BlockSpec((1, rows // 2, cols), lambda o, i, index: (index[o], i, 0))],
            out_specs=pl.BlockSpec((1, rows // 2, cols), lambda o, i, index: (o, i, 0)),
        ),
        compiler_params=pltpu.CompilerParams(vmem_limit_bytes=VMEM_LIMIT),
        cost_estimate=pl.CostEstimate(
            flops=0, bytes_accessed=2 * blocks.size * 2, transcendentals=0
        ),
    )(index, blocks)


def pair_kernel(
    tiles, slots, leads, follows, table, lead_ref, follow_ref, dipole_ref, out_ref, x_ref, xt_ref, m_ref
):
    tile = lead_ref.shape[1] // tiles
    half = lead_ref.shape[2]
    x_ref[:, :half] = lead_ref[0]
    x_ref[:, half:] = follow_ref[0]

    def project(r, carry):
        rows = pl.ds(pl.multiple_of(r * tile, tile), tile)
        picked = []
        for s in range(slots):
            col = table[r * slots + s]
            start = pl.multiple_of(jnp.maximum(col, 0) * tile, tile)
            piece = x_ref[pl.ds(start, tile), :]
            picked.append(jnp.where(col >= 0, piece, jnp.zeros_like(piece)))
        picked = jnp.concatenate(picked, axis=0)
        stacked = jnp.concatenate([dipole_ref[k, rows, :] for k in range(3)], axis=0)
        moments = jnp.dot(stacked, picked, preferred_element_type=jnp.float32)
        moments = moments.astype(jnp.bfloat16)
        for k in range(3):
            m_ref[k, rows, :] = moments[k * tile : (k + 1) * tile]
        xt_ref[:, rows] = x_ref[rows, :].T
        return carry

    lax.fori_loop(0, tiles, project, 0, unroll=4)
    upper = lax.broadcasted_iota(jnp.int32, (half, half), 0) <= lax.broadcasted_iota(
        jnp.int32, (half, half), 1
    )
    eye = lax.broadcasted_iota(jnp.int32, (half, half), 0) == lax.broadcasted_iota(
        jnp.int32, (half, half), 1
    )
    for k in range(3):
        gram = jnp.dot(xt_ref[...], m_ref[k], preferred_element_type=jnp.float32)
        gram = 0.5 * (gram + gram.T)
        tail = gram[half:, half:]
        diag = jnp.sum(jnp.where(eye, tail, 0.0), axis=0, keepdims=True)
        out_ref[0, k, :half] = gram[:half, half:]
        out_ref[0, k, half : 2 * half] = jnp.where(upper, gram[:half, :half], tail)
        out_ref[0, k, 2 * half :] = jnp.broadcast_to(diag, (8, half))


def pair_grams(local, dipole, table, leads, follows):
    blocks, rows, half = local.shape
    tiles, slots = table.shape
    pairs = blocks // 2
    flops = pairs * 2 * 3 * rows * 2 * half * (dipole.shape[2] + 2 * half)
    return pl.pallas_call(
        functools.partial(pair_kernel, tiles, slots),
        out_shape=jax.ShapeDtypeStruct((pairs, 3, 2 * half + 8, half), jnp.float32),
        grid_spec=pltpu.PrefetchScalarGridSpec(
            num_scalar_prefetch=3,
            grid=(pairs,),
            in_specs=[
                pl.BlockSpec((1, rows, half), lambda q, lead, follow, t: (lead[q], 0, 0)),
                pl.BlockSpec((1, rows, half), lambda q, lead, follow, t: (follow[q], 0, 0)),
                pl.BlockSpec(dipole.shape, lambda q, lead, follow, t: (0, 0, 0)),
            ],
            out_specs=pl.BlockSpec(
                (1, 3, 2 * half + 8, half), lambda q, lead, follow, t: (q, 0, 0, 0)
            ),
            scratch_shapes=[
                pltpu.VMEM((rows, 2 * half), jnp.bfloat16),
                pltpu.VMEM((2 * half, rows), jnp.bfloat16),
                pltpu.VMEM((3, rows, 2 * half), jnp.bfloat16),
            ],
        ),
        compiler_params=pltpu.CompilerParams(vmem_limit_bytes=VMEM_LIMIT),
        cost_estimate=pl.CostEstimate(
            flops=flops, bytes_accessed=2 * (local.size + dipole.size), transcendentals=0
        ),
    )(leads, follows, table.reshape(-1), local, local, dipole)


def arctan(x):
    mag = jnp.abs(x)
    big = mag > 2.414213562373095
    mid = mag > 0.4142135623730950
    num = jnp.where(big, -1.0, jnp.where(mid, mag - 1.0, mag))
    den = jnp.where(big, mag, jnp.where(mid, mag + 1.0, 1.0))
    base = jnp.where(big, 1.5707963267948966, jnp.where(mid, 0.7853981633974483, 0.0))
    t = num / den
    w = t * t
    poly = ((8.05374449538e-2 * w - 1.38776856032e-1) * w + 1.99777106478e-1) * w
    poly = (poly - 3.33329491539e-1) * w * t + t
    out = base + poly
    return jnp.where(x < 0, -out, out)


def jacobi_kernel(in_ref, out_ref):
    half = in_ref.shape[3]
    rows = lax.broadcasted_iota(jnp.int32, (half, half), 0)
    cols = lax.broadcasted_iota(jnp.int32, (half, half), 1)
    eye = rows == cols
    quads = []
    for k in range(3):
        cross = in_ref[0, k, :half]
        mixed = in_ref[0, k, half : 2 * half]
        flipped = mixed.T
        head = jnp.where(rows <= cols, mixed, flipped)
        tail = jnp.where(rows > cols, mixed, flipped)
        tail = jnp.where(eye, in_ref[0, k, 2 * half : 2 * half + 1], tail)
        quads.append([head, cross, cross.T, tail])
    one = jnp.where(eye, 1.0, 0.0).astype(jnp.float32)
    zero = jnp.zeros((half, half), jnp.float32)
    rotor = [one, zero, zero, one]

    def angles(axis):
        quad_term = lin_term = 0.0
        for ll, lf, _, ff in quads:
            head, off, tail = (
                jnp.sum(jnp.where(eye, v, 0.0), axis=axis, keepdims=True) for v in (ll, lf, ff)
            )
            spread = head - tail
            quad_term = quad_term + (off * off - 0.25 * spread * spread)
            lin_term = lin_term + off * spread
        theta = 0.25 * arctan(lin_term / (jnp.abs(quad_term) + 1.0))
        return jnp.cos(theta), jnp.sin(theta)

    for sweep in range(SWEEPS):
        if sweep:
            back = half - 1
            for q in quads:
                q[1] = pltpu.roll(q[1], back, 1)
                q[2] = pltpu.roll(q[2], back, 0)
                q[3] = pltpu.roll(pltpu.roll(q[3], back, 1), back, 0)
            rotor[1] = pltpu.roll(rotor[1], back, 1)
            rotor[3] = pltpu.roll(rotor[3], back, 1)
        row_cos, row_sin = angles(0)
        col_cos, col_sin = angles(1)
        for i, (ll, lf, fl, ff) in enumerate(quads):
            ll, lf = ll * row_cos + lf * row_sin, lf * row_cos - ll * row_sin
            fl, ff = fl * row_cos + ff * row_sin, ff * row_cos - fl * row_sin
            ll, fl = ll * col_cos + fl * col_sin, fl * col_cos - ll * col_sin
            lf, ff = lf * col_cos + ff * col_sin, ff * col_cos - lf * col_sin
            quads[i] = [ll, lf, fl, ff]
        ll, lf, fl, ff = rotor
        rotor = [
            ll * row_cos + lf * row_sin,
            lf * row_cos - ll * row_sin,
            fl * row_cos + ff * row_sin,
            ff * row_cos - fl * row_sin,
        ]
    lf, ff = (pltpu.roll(v, SWEEPS - 1, 1) for v in (rotor[1], rotor[3]))
    out_ref[0, :half, :half] = rotor[0].astype(jnp.bfloat16)
    out_ref[0, half:, :half] = rotor[2].astype(jnp.bfloat16)
    out_ref[0, :half, half:] = lf.astype(jnp.bfloat16)
    out_ref[0, half:, half:] = ff.astype(jnp.bfloat16)


def jacobi(grams):
    pairs, _, packed, half = grams.shape
    size = 2 * half
    return pl.pallas_call(
        jacobi_kernel,
        out_shape=jax.ShapeDtypeStruct((pairs, size, size), jnp.bfloat16),
        grid=(pairs,),
        in_specs=[pl.BlockSpec((1, 3, packed, half), lambda q: (q, 0, 0, 0))],
        out_specs=pl.BlockSpec((1, size, size), lambda q: (q, 0, 0)),
        compiler_params=pltpu.CompilerParams(vmem_limit_bytes=32 * 1024 * 1024),
        cost_estimate=pl.CostEstimate(
            flops=pairs * SWEEPS * 3 * 12 * size * size,
            bytes_accessed=grams.size * 4,
            transcendentals=pairs * SWEEPS * 4 * size,
        ),
    )(grams)


def rotate_kernel(own_ref, other_ref, weight_ref, out_ref):
    both = jnp.concatenate([own_ref[...], other_ref[...]], axis=1)
    out_ref[...] = jnp.dot(both, weight_ref[...], preferred_element_type=jnp.float32).astype(
        jnp.bfloat16
    )


def rotate(own, other, weight):
    rows, half = own.shape
    step = min(rows, 2048)
    return pl.pallas_call(
        rotate_kernel,
        out_shape=jax.ShapeDtypeStruct(own.shape, own.dtype),
        grid=(rows // step,),
        in_specs=[
            pl.BlockSpec((step, half), lambda i: (i, 0)),
            pl.BlockSpec((step, half), lambda i: (i, 0)),
            pl.BlockSpec((2 * half, half), lambda i: (0, 0)),
        ],
        out_specs=pl.BlockSpec((step, half), lambda i: (i, 0)),
        compiler_params=pltpu.CompilerParams(vmem_limit_bytes=VMEM_LIMIT),
        cost_estimate=pl.CostEstimate(
            flops=4 * rows * half * half, bytes_accessed=6 * own.size, transcendentals=0
        ),
    )(own, other, weight)


def body(coeffs, dipole, tile_cols, matching):
    blocks = lax.axis_size("orb")
    me = lax.axis_index("orb")
    rows, half = coeffs.shape
    pairs = blocks // 2
    block_ids = jnp.arange(blocks, dtype=jnp.int32)
    partner = matching[0]
    is_lead = block_ids < partner
    before = is_lead[None, :] & (block_ids[None, :] < block_ids[:, None])
    rank = jnp.sum(before.astype(jnp.int32), axis=1)
    chosen = is_lead[None, :] & (rank[None, :] == jnp.arange(pairs, dtype=jnp.int32)[:, None])
    leads = jnp.sum(jnp.where(chosen, block_ids[None, :], 0), axis=1)
    follows = jnp.sum(jnp.where(chosen, partner[None, :], 0), axis=1)

    local = lax.all_to_all(
        coeffs.reshape(blocks, rows // blocks, half), "orb", split_axis=0, concat_axis=0
    )
    swapped = permute_blocks(local, partner)
    other = lax.all_to_all(swapped, "orb", split_axis=0, concat_axis=0).reshape(rows, half)

    grams = pair_grams(local, dipole[:, 0], tile_cols[0], leads, follows)
    grams = lax.psum_scatter(grams, "bas", scatter_dimension=0, tiled=True)
    grams = lax.psum(grams, "orb")
    rotors = lax.all_gather(jacobi(grams), "bas", axis=0, tiled=True)
    mine = (leads == me) | (follows == me)
    rotor = jnp.sum(jnp.where(mine[:, None, None], rotors, jnp.zeros_like(rotors)), axis=0)
    leading = jnp.any(leads == me)
    weight = jnp.where(
        leading,
        rotor[:, :half],
        jnp.concatenate([rotor[half:, half:], rotor[:half, half:]], axis=0),
    )
    return rotate(coeffs, other, weight)


def solution(mesh):
    in_specs = (P("bas", "orb"), P(None, "bas", "orb", None), P("bas", "orb", None), P())
    out_specs = P("bas", "orb")
    return jax.shard_map(body, mesh=mesh, in_specs=in_specs, out_specs=out_specs, check_vma=False)
```

```python
import functools

import jax
import jax.numpy as jnp
from jax import lax
from jax.experimental import pallas as pl
from jax.experimental.pallas import tpu as pltpu
from jax.sharding import PartitionSpec as P

SWEEPS = 4
VMEM_LIMIT = 56 * 1024 * 1024


def permute_kernel(index_ref, in_ref, out_ref):
    out_ref[...] = in_ref[...]


def permute_blocks(blocks, index, start, size):
    count, _, cols = blocks.shape
    return pl.pallas_call(
        permute_kernel,
        out_shape=jax.ShapeDtypeStruct((count, size, cols), blocks.dtype),
        grid_spec=pltpu.PrefetchScalarGridSpec(
            num_scalar_prefetch=1,
            grid=(count,),
            in_specs=[
                pl.BlockSpec((1, size, cols), lambda o, index: (index[o], start // size, 0))
            ],
            out_specs=pl.BlockSpec((1, size, cols), lambda o, index: (o, 0, 0)),
        ),
        compiler_params=pltpu.CompilerParams(vmem_limit_bytes=VMEM_LIMIT),
        cost_estimate=pl.CostEstimate(
            flops=0, bytes_accessed=4 * count * size * cols, transcendentals=0
        ),
    )(index, blocks)


def pair_kernel(
    tiles, slots, leads, follows, table, lead_ref, follow_ref, dipole_ref, out_ref, x_ref, xt_ref, m_ref
):
    tile = lead_ref.shape[1] // tiles
    half = lead_ref.shape[2]
    x_ref[:, :half] = lead_ref[0]
    x_ref[:, half:] = follow_ref[0]

    def project(r, carry):
        rows = pl.ds(pl.multiple_of(r * tile, tile), tile)
        picked = []
        for s in range(slots):
            col = table[r * slots + s]
            start = pl.multiple_of(jnp.maximum(col, 0) * tile, tile)
            piece = x_ref[pl.ds(start, tile), :]
            picked.append(jnp.where(col >= 0, piece, jnp.zeros_like(piece)))
        picked = jnp.concatenate(picked, axis=0)
        stacked = jnp.concatenate([dipole_ref[k, rows, :] for k in range(3)], axis=0)
        moments = jnp.dot(stacked, picked, preferred_element_type=jnp.float32)
        moments = moments.astype(jnp.bfloat16)
        for k in range(3):
            m_ref[k, rows, :] = moments[k * tile : (k + 1) * tile]
        xt_ref[:, rows] = x_ref[rows, :].T
        return carry

    lax.fori_loop(0, tiles, project, 0, unroll=4)
    upper = lax.broadcasted_iota(jnp.int32, (half, half), 0) <= lax.broadcasted_iota(
        jnp.int32, (half, half), 1
    )
    eye = lax.broadcasted_iota(jnp.int32, (half, half), 0) == lax.broadcasted_iota(
        jnp.int32, (half, half), 1
    )
    for k in range(3):
        gram = jnp.dot(xt_ref[...], m_ref[k], preferred_element_type=jnp.float32)
        gram = 0.5 * (gram + gram.T)
        tail = gram[half:, half:]
        diag = jnp.sum(jnp.where(eye, tail, 0.0), axis=0, keepdims=True)
        out_ref[0, k, :half] = gram[:half, half:]
        out_ref[0, k, half : 2 * half] = jnp.where(upper, gram[:half, :half], tail)
        out_ref[0, k, 2 * half :] = jnp.broadcast_to(diag, (8, half))


def pair_grams(local, dipole, table, leads, follows):
    blocks, rows, half = local.shape
    tiles, slots = table.shape
    pairs = blocks // 2
    flops = pairs * 2 * 3 * rows * 2 * half * (dipole.shape[2] + 2 * half)
    return pl.pallas_call(
        functools.partial(pair_kernel, tiles, slots),
        out_shape=jax.ShapeDtypeStruct((pairs, 3, 2 * half + 8, half), jnp.float32),
        grid_spec=pltpu.PrefetchScalarGridSpec(
            num_scalar_prefetch=3,
            grid=(pairs,),
            in_specs=[
                pl.BlockSpec((1, rows, half), lambda q, lead, follow, t: (lead[q], 0, 0)),
                pl.BlockSpec((1, rows, half), lambda q, lead, follow, t: (follow[q], 0, 0)),
                pl.BlockSpec(dipole.shape, lambda q, lead, follow, t: (0, 0, 0)),
            ],
            out_specs=pl.BlockSpec(
                (1, 3, 2 * half + 8, half), lambda q, lead, follow, t: (q, 0, 0, 0)
            ),
            scratch_shapes=[
                pltpu.VMEM((rows, 2 * half), jnp.bfloat16),
                pltpu.VMEM((2 * half, rows), jnp.bfloat16),
                pltpu.VMEM((3, rows, 2 * half), jnp.bfloat16),
            ],
        ),
        compiler_params=pltpu.CompilerParams(vmem_limit_bytes=VMEM_LIMIT),
        cost_estimate=pl.CostEstimate(
            flops=flops, bytes_accessed=2 * (local.size + dipole.size), transcendentals=0
        ),
    )(leads, follows, table.reshape(-1), local, local, dipole)


def arctan(x):
    mag = jnp.abs(x)
    big = mag > 2.414213562373095
    mid = mag > 0.4142135623730950
    num = jnp.where(big, -1.0, jnp.where(mid, mag - 1.0, mag))
    den = jnp.where(big, mag, jnp.where(mid, mag + 1.0, 1.0))
    base = jnp.where(big, 1.5707963267948966, jnp.where(mid, 0.7853981633974483, 0.0))
    t = num / den
    w = t * t
    poly = ((8.05374449538e-2 * w - 1.38776856032e-1) * w + 1.99777106478e-1) * w
    poly = (poly - 3.33329491539e-1) * w * t + t
    out = base + poly
    return jnp.where(x < 0, -out, out)


def jacobi_kernel(in_ref, out_ref):
    half = in_ref.shape[3]
    rows = lax.broadcasted_iota(jnp.int32, (half, half), 0)
    cols = lax.broadcasted_iota(jnp.int32, (half, half), 1)
    eye = rows == cols
    quads = []
    for k in range(3):
        cross = in_ref[0, k, :half]
        mixed = in_ref[0, k, half : 2 * half]
        flipped = mixed.T
        head = jnp.where(rows <= cols, mixed, flipped)
        tail = jnp.where(rows > cols, mixed, flipped)
        tail = jnp.where(eye, in_ref[0, k, 2 * half : 2 * half + 1], tail)
        quads.append([head, cross, cross.T, tail])
    one = jnp.where(eye, 1.0, 0.0).astype(jnp.float32)
    zero = jnp.zeros((half, half), jnp.float32)
    rotor = [one, zero, zero, one]

    def angles(axis):
        quad_term = lin_term = 0.0
        for ll, lf, _, ff in quads:
            head, off, tail = (
                jnp.sum(jnp.where(eye, v, 0.0), axis=axis, keepdims=True) for v in (ll, lf, ff)
            )
            spread = head - tail
            quad_term = quad_term + (off * off - 0.25 * spread * spread)
            lin_term = lin_term + off * spread
        theta = 0.25 * arctan(lin_term / (jnp.abs(quad_term) + 1.0))
        return jnp.cos(theta), jnp.sin(theta)

    for sweep in range(SWEEPS):
        if sweep:
            back = half - 1
            for q in quads:
                q[1] = pltpu.roll(q[1], back, 1)
                q[2] = pltpu.roll(q[2], back, 0)
                q[3] = pltpu.roll(pltpu.roll(q[3], back, 1), back, 0)
            rotor[1] = pltpu.roll(rotor[1], back, 1)
            rotor[3] = pltpu.roll(rotor[3], back, 1)
        row_cos, row_sin = angles(0)
        col_cos, col_sin = angles(1)
        for i, (ll, lf, fl, ff) in enumerate(quads):
            ll, lf = ll * row_cos + lf * row_sin, lf * row_cos - ll * row_sin
            fl, ff = fl * row_cos + ff * row_sin, ff * row_cos - fl * row_sin
            ll, fl = ll * col_cos + fl * col_sin, fl * col_cos - ll * col_sin
            lf, ff = lf * col_cos + ff * col_sin, ff * col_cos - lf * col_sin
            quads[i] = [ll, lf, fl, ff]
        ll, lf, fl, ff = rotor
        rotor = [
            ll * row_cos + lf * row_sin,
            lf * row_cos - ll * row_sin,
            fl * row_cos + ff * row_sin,
            ff * row_cos - fl * row_sin,
        ]
    lf, ff = (pltpu.roll(v, SWEEPS - 1, 1) for v in (rotor[1], rotor[3]))
    out_ref[0, :half, :half] = rotor[0].astype(jnp.bfloat16)
    out_ref[0, half:, :half] = rotor[2].astype(jnp.bfloat16)
    out_ref[0, :half, half:] = lf.astype(jnp.bfloat16)
    out_ref[0, half:, half:] = ff.astype(jnp.bfloat16)


def jacobi(grams):
    pairs, _, packed, half = grams.shape
    size = 2 * half
    return pl.pallas_call(
        jacobi_kernel,
        out_shape=jax.ShapeDtypeStruct((pairs, size, size), jnp.bfloat16),
        grid=(pairs,),
        in_specs=[pl.BlockSpec((1, 3, packed, half), lambda q: (q, 0, 0, 0))],
        out_specs=pl.BlockSpec((1, size, size), lambda q: (q, 0, 0)),
        compiler_params=pltpu.CompilerParams(vmem_limit_bytes=32 * 1024 * 1024),
        cost_estimate=pl.CostEstimate(
            flops=pairs * SWEEPS * 3 * 12 * size * size,
            bytes_accessed=grams.size * 4,
            transcendentals=pairs * SWEEPS * 4 * size,
        ),
    )(grams)


def rotate_kernel(own_ref, other_ref, weight_ref, *refs):
    out_ref = refs[-1]
    count, rows, half = own_ref.shape
    both = jnp.concatenate([own_ref[...], other_ref[...]], axis=2).reshape(count * rows, 2 * half)
    out = jnp.dot(both, weight_ref[...], preferred_element_type=jnp.float32)
    out_ref[...] = out.astype(jnp.bfloat16).reshape(count, rows, half)


def rotate(own, other, weight, start, size, step, done=None):
    groups, _, half = own.shape
    at = start // size
    return pl.pallas_call(
        rotate_kernel,
        out_shape=jax.ShapeDtypeStruct(own.shape, own.dtype),
        grid=(groups // step,),
        in_specs=[
            pl.BlockSpec((step, size, half), lambda i: (i, at, 0)),
            pl.BlockSpec((step, size, half), lambda i: (i, 0, 0)),
            pl.BlockSpec((2 * half, half), lambda i: (0, 0)),
        ]
        + ([] if done is None else [pl.BlockSpec(memory_space=pl.ANY)]),
        out_specs=pl.BlockSpec((step, size, half), lambda i: (i, at, 0)),
        input_output_aliases={} if done is None else {3: 0},
        compiler_params=pltpu.CompilerParams(vmem_limit_bytes=VMEM_LIMIT),
        cost_estimate=pl.CostEstimate(
            flops=4 * groups * size * half * half,
            bytes_accessed=6 * groups * size * half,
            transcendentals=0,
        ),
    )(own, other, weight, *([] if done is None else [done]))


def body(coeffs, dipole, tile_cols, matching):
    blocks = lax.axis_size("orb")
    me = lax.axis_index("orb")
    rows, half = coeffs.shape
    pairs = blocks // 2
    block_ids = jnp.arange(blocks, dtype=jnp.int32)
    partner = matching[0]
    is_lead = block_ids < partner
    before = is_lead[None, :] & (block_ids[None, :] < block_ids[:, None])
    rank = jnp.sum(before.astype(jnp.int32), axis=1)
    chosen = is_lead[None, :] & (rank[None, :] == jnp.arange(pairs, dtype=jnp.int32)[:, None])
    leads = jnp.sum(jnp.where(chosen, block_ids[None, :], 0), axis=1)
    follows = jnp.sum(jnp.where(chosen, partner[None, :], 0), axis=1)

    own = coeffs.reshape(blocks, rows // blocks, half)
    last = rows // blocks // 4
    first = 3 * last
    local = lax.all_to_all(own, "orb", split_axis=0, concat_axis=0)
    swapped = permute_blocks(local, partner, 0, first)
    other_first = lax.all_to_all(swapped, "orb", split_axis=0, concat_axis=0)

    grams = pair_grams(local, dipole[:, 0], tile_cols[0], leads, follows)
    grams = lax.psum_scatter(grams, "bas", scatter_dimension=0, tiled=True)
    grams = lax.psum(grams, "orb")
    swapped = permute_blocks(local, partner, first, last)
    swapped, grams = lax.optimization_barrier((swapped, grams))
    other_last = lax.all_to_all(swapped, "orb", split_axis=0, concat_axis=0)
    rotors = lax.all_gather(jacobi(grams), "bas", axis=0, tiled=True)
    mine = (leads == me) | (follows == me)
    rotor = jnp.sum(jnp.where(mine[:, None, None], rotors, jnp.zeros_like(rotors)), axis=0)
    leading = jnp.any(leads == me)
    weight = jnp.where(
        leading,
        rotor[:, :half],
        jnp.concatenate([rotor[half:, half:], rotor[:half, half:]], axis=0),
    )
    out = rotate(own, other_first, weight, 0, first, 1)
    out = rotate(own, other_last, weight, first, last, blocks // 2, out)
    return out.reshape(rows, half)


def solution(mesh):
    in_specs = (P("bas", "orb"), P(None, "bas", "orb", None), P("bas", "orb", None), P())
    out_specs = P("bas", "orb")
    return jax.shard_map(body, mesh=mesh, in_specs=in_specs, out_specs=out_specs, check_vma=False)
```

```python
import functools

import jax
import jax.numpy as jnp
from jax import lax
from jax.experimental import pallas as pl
from jax.experimental.pallas import tpu as pltpu
from jax.sharding import PartitionSpec as P

SWEEPS = 4
VMEM_LIMIT = 56 * 1024 * 1024


def permute_kernel(index_ref, in_ref, out_ref):
    out_ref[...] = in_ref[...]


def permute_blocks(blocks, index, start, size):
    count, _, cols = blocks.shape
    return pl.pallas_call(
        permute_kernel,
        out_shape=jax.ShapeDtypeStruct((count, size, cols), blocks.dtype),
        grid_spec=pltpu.PrefetchScalarGridSpec(
            num_scalar_prefetch=1,
            grid=(count,),
            in_specs=[
                pl.BlockSpec((1, size, cols), lambda o, index: (index[o], start // size, 0))
            ],
            out_specs=pl.BlockSpec((1, size, cols), lambda o, index: (o, 0, 0)),
        ),
        compiler_params=pltpu.CompilerParams(vmem_limit_bytes=VMEM_LIMIT),
        cost_estimate=pl.CostEstimate(
            flops=0, bytes_accessed=4 * count * size * cols, transcendentals=0
        ),
    )(index, blocks)


def pair_kernel(
    tiles, slots, leads, follows, table, lead_ref, follow_ref, dipole_ref, out_ref, x_ref, xt_ref, m_ref
):
    tile = lead_ref.shape[1] // tiles
    half = lead_ref.shape[2]
    x_ref[:, :half] = lead_ref[0]
    x_ref[:, half:] = follow_ref[0]

    def project(r, carry):
        rows = pl.ds(pl.multiple_of(r * tile, tile), tile)
        picked = []
        for s in range(slots):
            col = table[r * slots + s]
            start = pl.multiple_of(jnp.maximum(col, 0) * tile, tile)
            piece = x_ref[pl.ds(start, tile), :]
            picked.append(jnp.where(col >= 0, piece, jnp.zeros_like(piece)))
        picked = jnp.concatenate(picked, axis=0)
        stacked = jnp.concatenate([dipole_ref[k, rows, :] for k in range(3)], axis=0)
        moments = jnp.dot(stacked, picked, preferred_element_type=jnp.float32)
        moments = moments.astype(jnp.bfloat16)
        for k in range(3):
            m_ref[k, rows, :] = moments[k * tile : (k + 1) * tile]
        xt_ref[:, rows] = x_ref[rows, :].T
        return carry

    lax.fori_loop(0, tiles, project, 0, unroll=4)
    upper = lax.broadcasted_iota(jnp.int32, (half, half), 0) <= lax.broadcasted_iota(
        jnp.int32, (half, half), 1
    )
    eye = lax.broadcasted_iota(jnp.int32, (half, half), 0) == lax.broadcasted_iota(
        jnp.int32, (half, half), 1
    )
    for k in range(3):
        gram = jnp.dot(xt_ref[...], m_ref[k], preferred_element_type=jnp.float32)
        gram = 0.5 * (gram + gram.T)
        tail = gram[half:, half:]
        diag = jnp.sum(jnp.where(eye, tail, 0.0), axis=0, keepdims=True)
        out_ref[0, k, :half] = gram[:half, half:]
        out_ref[0, k, half : 2 * half] = jnp.where(upper, gram[:half, :half], tail)
        out_ref[0, k, 2 * half :] = jnp.broadcast_to(diag, (8, half))


def pair_grams(local, dipole, table, leads, follows):
    blocks, rows, half = local.shape
    tiles, slots = table.shape
    pairs = blocks // 2
    flops = pairs * 2 * 3 * rows * 2 * half * (dipole.shape[2] + 2 * half)
    return pl.pallas_call(
        functools.partial(pair_kernel, tiles, slots),
        out_shape=jax.ShapeDtypeStruct((pairs, 3, 2 * half + 8, half), jnp.float32),
        grid_spec=pltpu.PrefetchScalarGridSpec(
            num_scalar_prefetch=3,
            grid=(pairs,),
            in_specs=[
                pl.BlockSpec((1, rows, half), lambda q, lead, follow, t: (lead[q], 0, 0)),
                pl.BlockSpec((1, rows, half), lambda q, lead, follow, t: (follow[q], 0, 0)),
                pl.BlockSpec(dipole.shape, lambda q, lead, follow, t: (0, 0, 0)),
            ],
            out_specs=pl.BlockSpec(
                (1, 3, 2 * half + 8, half), lambda q, lead, follow, t: (q, 0, 0, 0)
            ),
            scratch_shapes=[
                pltpu.VMEM((rows, 2 * half), jnp.bfloat16),
                pltpu.VMEM((2 * half, rows), jnp.bfloat16),
                pltpu.VMEM((3, rows, 2 * half), jnp.bfloat16),
            ],
        ),
        compiler_params=pltpu.CompilerParams(vmem_limit_bytes=VMEM_LIMIT),
        cost_estimate=pl.CostEstimate(
            flops=flops, bytes_accessed=2 * (local.size + dipole.size), transcendentals=0
        ),
    )(leads, follows, table.reshape(-1), local, local, dipole)


def arctan(x):
    mag = jnp.abs(x)
    big = mag > 2.414213562373095
    mid = mag > 0.4142135623730950
    num = jnp.where(big, -1.0, jnp.where(mid, mag - 1.0, mag))
    den = jnp.where(big, mag, jnp.where(mid, mag + 1.0, 1.0))
    base = jnp.where(big, 1.5707963267948966, jnp.where(mid, 0.7853981633974483, 0.0))
    t = num / den
    w = t * t
    poly = ((8.05374449538e-2 * w - 1.38776856032e-1) * w + 1.99777106478e-1) * w
    poly = (poly - 3.33329491539e-1) * w * t + t
    out = base + poly
    return jnp.where(x < 0, -out, out)


def jacobi_kernel(in_ref, out_ref):
    half = in_ref.shape[3]
    rows = lax.broadcasted_iota(jnp.int32, (half, half), 0)
    cols = lax.broadcasted_iota(jnp.int32, (half, half), 1)
    eye = rows == cols
    quads = []
    for k in range(3):
        cross = in_ref[0, k, :half]
        mixed = in_ref[0, k, half : 2 * half]
        flipped = mixed.T
        head = jnp.where(rows <= cols, mixed, flipped)
        tail = jnp.where(rows > cols, mixed, flipped)
        tail = jnp.where(eye, in_ref[0, k, 2 * half : 2 * half + 1], tail)
        quads.append([head, cross, cross.T, tail])
    one = jnp.where(eye, 1.0, 0.0).astype(jnp.float32)
    zero = jnp.zeros((half, half), jnp.float32)
    rotor = [one, zero, zero, one]

    def angles(axis):
        quad_term = lin_term = 0.0
        for ll, lf, _, ff in quads:
            head, off, tail = (
                jnp.sum(jnp.where(eye, v, 0.0), axis=axis, keepdims=True) for v in (ll, lf, ff)
            )
            spread = head - tail
            quad_term = quad_term + (off * off - 0.25 * spread * spread)
            lin_term = lin_term + off * spread
        theta = 0.25 * arctan(lin_term / (jnp.abs(quad_term) + 1.0))
        return jnp.cos(theta), jnp.sin(theta)

    for sweep in range(SWEEPS):
        if sweep:
            back = half - 1
            for q in quads:
                q[1] = pltpu.roll(q[1], back, 1)
                q[2] = pltpu.roll(q[2], back, 0)
                q[3] = pltpu.roll(pltpu.roll(q[3], back, 1), back, 0)
            rotor[1] = pltpu.roll(rotor[1], back, 1)
            rotor[3] = pltpu.roll(rotor[3], back, 1)
        row_cos, row_sin = angles(0)
        col_cos, col_sin = angles(1)
        for i, (ll, lf, fl, ff) in enumerate(quads):
            ll, lf = ll * row_cos + lf * row_sin, lf * row_cos - ll * row_sin
            fl, ff = fl * row_cos + ff * row_sin, ff * row_cos - fl * row_sin
            ll, fl = ll * col_cos + fl * col_sin, fl * col_cos - ll * col_sin
            lf, ff = lf * col_cos + ff * col_sin, ff * col_cos - lf * col_sin
            quads[i] = [ll, lf, fl, ff]
        ll, lf, fl, ff = rotor
        rotor = [
            ll * row_cos + lf * row_sin,
            lf * row_cos - ll * row_sin,
            fl * row_cos + ff * row_sin,
            ff * row_cos - fl * row_sin,
        ]
    lf, ff = (pltpu.roll(v, SWEEPS - 1, 1) for v in (rotor[1], rotor[3]))
    out_ref[0, :half, :half] = rotor[0].astype(jnp.bfloat16)
    out_ref[0, half:, :half] = rotor[2].astype(jnp.bfloat16)
    out_ref[0, :half, half:] = lf.astype(jnp.bfloat16)
    out_ref[0, half:, half:] = ff.astype(jnp.bfloat16)


def jacobi(grams):
    pairs, _, packed, half = grams.shape
    size = 2 * half
    return pl.pallas_call(
        jacobi_kernel,
        out_shape=jax.ShapeDtypeStruct((pairs, size, size), jnp.bfloat16),
        grid=(pairs,),
        in_specs=[pl.BlockSpec((1, 3, packed, half), lambda q: (q, 0, 0, 0))],
        out_specs=pl.BlockSpec((1, size, size), lambda q: (q, 0, 0)),
        compiler_params=pltpu.CompilerParams(vmem_limit_bytes=32 * 1024 * 1024),
        cost_estimate=pl.CostEstimate(
            flops=pairs * SWEEPS * 3 * 12 * size * size,
            bytes_accessed=grams.size * 4,
            transcendentals=pairs * SWEEPS * 4 * size,
        ),
    )(grams)


def rotate_kernel(own_ref, other_ref, weight_ref, *refs):
    out_ref = refs[-1]
    count, rows, half = own_ref.shape
    both = jnp.concatenate([own_ref[...], other_ref[...]], axis=2).reshape(count * rows, 2 * half)
    out = jnp.dot(both, weight_ref[...], preferred_element_type=jnp.float32)
    out_ref[...] = out.astype(jnp.bfloat16).reshape(count, rows, half)


def rotate(own, other, weight, start, size, step, done=None):
    groups, _, half = own.shape
    at = start // size
    return pl.pallas_call(
        rotate_kernel,
        out_shape=jax.ShapeDtypeStruct(own.shape, own.dtype),
        grid=(groups // step,),
        in_specs=[
            pl.BlockSpec((step, size, half), lambda i: (i, at, 0)),
            pl.BlockSpec((step, size, half), lambda i: (i, 0, 0)),
            pl.BlockSpec((2 * half, half), lambda i: (0, 0)),
        ]
        + ([] if done is None else [pl.BlockSpec(memory_space=pl.ANY)]),
        out_specs=pl.BlockSpec((step, size, half), lambda i: (i, at, 0)),
        input_output_aliases={} if done is None else {3: 0},
        compiler_params=pltpu.CompilerParams(vmem_limit_bytes=VMEM_LIMIT),
        cost_estimate=pl.CostEstimate(
            flops=4 * groups * size * half * half,
            bytes_accessed=6 * groups * size * half,
            transcendentals=0,
        ),
    )(own, other, weight, *([] if done is None else [done]))


def body(coeffs, dipole, tile_cols, matching):
    blocks = lax.axis_size("orb")
    me = lax.axis_index("orb")
    rows, half = coeffs.shape
    pairs = blocks // 2
    block_ids = jnp.arange(blocks, dtype=jnp.int32)
    partner = matching[0]
    is_lead = block_ids < partner
    before = is_lead[None, :] & (block_ids[None, :] < block_ids[:, None])
    rank = jnp.sum(before.astype(jnp.int32), axis=1)
    chosen = is_lead[None, :] & (rank[None, :] == jnp.arange(pairs, dtype=jnp.int32)[:, None])
    leads = jnp.sum(jnp.where(chosen, block_ids[None, :], 0), axis=1)
    follows = jnp.sum(jnp.where(chosen, partner[None, :], 0), axis=1)

    own = coeffs.reshape(blocks, rows // blocks, half)
    last = rows // blocks // 8
    first = 7 * last
    local = lax.all_to_all(own, "orb", split_axis=0, concat_axis=0)
    swapped = permute_blocks(local, partner, 0, first)
    other_first = lax.all_to_all(swapped, "orb", split_axis=0, concat_axis=0)

    grams = pair_grams(local, dipole[:, 0], tile_cols[0], leads, follows)
    grams = lax.psum_scatter(grams, "bas", scatter_dimension=0, tiled=True)
    grams = lax.psum(grams, "orb")
    swapped = permute_blocks(local, partner, first, last)
    swapped, grams = lax.optimization_barrier((swapped, grams))
    other_last = lax.all_to_all(swapped, "orb", split_axis=0, concat_axis=0)
    rotors = lax.all_gather(jacobi(grams), "bas", axis=0, tiled=True)
    mine = (leads == me) | (follows == me)
    rotor = jnp.sum(jnp.where(mine[:, None, None], rotors, jnp.zeros_like(rotors)), axis=0)
    leading = jnp.any(leads == me)
    weight = jnp.where(
        leading,
        rotor[:, :half],
        jnp.concatenate([rotor[half:, half:], rotor[:half, half:]], axis=0),
    )
    out = rotate(own, other_first, weight, 0, first, 1)
    out = rotate(own, other_last, weight, first, last, blocks // 2, out)
    return out.reshape(rows, half)


def solution(mesh):
    in_specs = (P("bas", "orb"), P(None, "bas", "orb", None), P("bas", "orb", None), P())
    out_specs = P("bas", "orb")
    return jax.shard_map(body, mesh=mesh, in_specs=in_specs, out_specs=out_specs, check_vma=False)
```
